256 devices in a mesh: task: 32 (over z, x), tp: 8 (over y, core).
Axes of the slice: x: 4, y: 4, z: 8, core: 2. Of those that a mesh axis runs over, the one named last changes fastest.
Arguments:
- queries: bfloat16 [3072, 8192], P('task', 'tp'), may hold values from -110 to 110
- prompt_keys: bfloat16 [131072, 1024], P('task', 'tp'), may hold values from -6 to 6
- prompt_values: bfloat16 [131072, 1024], P('task', 'tp'), may hold values from -6 to 6
- suffix_keys: bfloat16 [262144, 1024], P('task', 'tp'), may hold values from -6 to 6
- suffix_values: bfloat16 [262144, 1024], P('task', 'tp'), may hold values from -6 to 6
- new_keys: bfloat16 [3072, 1024], P('task', 'tp'), may hold values from -6 to 6
- new_values: bfloat16 [3072, 1024], P('task', 'tp'), may hold values from -6 to 6
- out_weight: bfloat16 [8192, 8192], P('tp', 'task'), may hold values from -0.5 to 0.5
- span_perm: int32 [512], P('task'), may hold values from 0 to 511, each once
- share_counts: int32 [16], replicated, may hold values from 1 to 160, 1024 in all
- sample_perm: int32 [1024], replicated, may hold values from 0 to 1023, each once
- decoded_lens: int32 [1024], P('task'), may hold values from 1 to 256, as said below
Outputs:
- head_mix: float32 [3072, 8192], P('tp', 'task')
The draws below stay inside these ranges and needn't reach their ends.
Inputs may be any that keep to these rules, and one draw needn't show every extreme that they name: `decoded_lens`: every sample has decoded at least one token; some sample has filled all 256 slots. `share_counts`: the counts sum to 1024; some prompt has exactly 160 samples. `span_perm`: every prompt block stands in exactly one task slot.
All inputs are finite; a program needn't handle non-finite values.
Results may differ from the reference program's by a relative error of at most 0.008.
Values may be sent and summed in bfloat16 or wider, within the bound.
A program may use at most 128 MiB of HBM per device.

```python
import math
import jax
import jax.numpy as jnp
import numpy as np
from jax import lax

D = 8192
H = 64
KVH = 8
HD = 128
PLEN = 8192
SPAN = 256
MAXSHARE = 160
SUF = 256
SPANS = 512
PROMPTS = 16
SAMPLES = 1024


def draw_queries(key, part):
    key = jax.random.fold_in(key, 11)
    first_key = jax.random.fold_in(key, 0)
    row_count = SAMPLES * 3
    values = jnp.clip(2.0 * jax.random.normal(first_key, (row_count, H * HD), jnp.float32), -16.0, 16.0)
    return values.astype(jnp.bfloat16)


def draw_decoded_lens(key, part):
    key = jax.random.fold_in(key, 23)
    first_key, second_key = jax.random.split(key)
    lengths = jax.random.randint(first_key, (SAMPLES,), 1, SUF + 1, dtype=jnp.int32)
    filled = jax.random.randint(second_key, (), 0, SAMPLES, dtype=jnp.int32)
    return lengths.at[filled].set(SUF).astype(jnp.int32)


def shard_levels(key, extent, cuts, least, high):
    def one(dim, blocks):
        heights = jax.random.uniform(jax.random.fold_in(jax.random.fold_in(key, 6), dim), (blocks,), jnp.float32, least / len(cuts), high / len(cuts))
        return jnp.repeat(jnp.exp(heights), extent[dim] // blocks).reshape((-1,) + (1,) * (len(extent) - dim - 1))

    loudness = one(*cuts[0])
    for cut in cuts[1:]:
        loudness = loudness * one(*cut)
    return loudness


def profile(amount, total, most, skew):
    loads = [(1 << 20) // math.isqrt(grade ** skew) + 1 for grade in range(2, amount + 1)]
    surplus, given = total - most - (amount - 1), [1] * (amount - 1)
    while surplus > 0:
        candidates = [i for i in range(amount - 1) if given[i] < most]
        whole, budget = sum([loads[i] for i in candidates]), surplus
        for i in candidates:
            extra = min(most - given[i], max(1, budget * loads[i] // whole), surplus)
            given[i] = given[i] + extra
            surplus = surplus - extra
    return np.array([most] + given)


def ragged_sizes(stream_key, number_of, total, limit, lean):
    if number_of == 2:
        one = jax.random.randint(stream_key, (), max(1, total - limit), min(limit, total - 1) + 1)
        return jnp.stack([one, total - one])
    sizes = jnp.asarray(profile(number_of, total, limit, lean), jnp.int32)
    couples = (number_of - 1) // 2
    donor, receiver = sizes[1:1 + 2 * couples:2], sizes[2:2 + 2 * couples:2]
    margin = jnp.minimum(donor - 1, limit - receiver)
    shifted = jax.random.randint(jax.random.fold_in(stream_key, 1), (couples,), 0, 1 << 20) % (margin + 1)
    sizes = sizes.at[1:1 + 2 * couples:2].set(donor - shifted).at[2:2 + 2 * couples:2].set(receiver + shifted)
    return sizes[jax.random.permutation(jax.random.fold_in(stream_key, 2), number_of)]


def gaussian(stream_key, shape, spread, bound, shards=(), kind=jnp.bfloat16):
    loudness = shard_levels(stream_key, shape, shards, -0.22, 0.18) if shards else 1.0
    values = jax.random.normal(stream_key, shape, jnp.float32) * spread * loudness
    return jnp.minimum(jnp.maximum(values, -bound), bound).astype(kind)


def setup_inputs(seed: int = 0) -> dict:
    seeds = jax.random.split(jax.random.key(seed), 13)
    queries = draw_queries(jax.random.fold_in(seeds[12], 71), 0)
    prompt_keys = gaussian(seeds[1], (SPANS * SPAN, KVH * HD), 1.0, 6.0, ((0, 32), (1, 8)))
    prompt_values = gaussian(seeds[2], (SPANS * SPAN, KVH * HD), 1.0, 6.0, ((0, 32), (1, 8)))
    suffix_keys = gaussian(seeds[3], (SAMPLES * SUF, KVH * HD), 1.0, 6.0, ((0, 32), (1, 8)))
    suffix_values = gaussian(seeds[4], (SAMPLES * SUF, KVH * HD), 1.0, 6.0, ((0, 32), (1, 8)))
    new_keys = gaussian(seeds[5], (SAMPLES * 3, KVH * HD), 1.0, 6.0, ((0, 32), (1, 8)))
    new_values = gaussian(seeds[6], (SAMPLES * 3, KVH * HD), 1.0, 6.0, ((0, 32), (1, 8)))
    out_weight = gaussian(seeds[7], (H * HD, D), (H * HD // 64) ** -0.5, 0.5, ((0, 8), (1, 32)))
    span_perm = jax.random.permutation(seeds[8], SPANS).astype(jnp.int32)
    share_counts = ragged_sizes(seeds[9], PROMPTS, SAMPLES, MAXSHARE, 2).astype(jnp.int32)
    sample_perm = jax.random.permutation(seeds[10], SAMPLES).astype(jnp.int32)
    decoded_lens = draw_decoded_lens(jax.random.fold_in(seeds[12], 71), 0)
    return {"queries": queries, "prompt_keys": prompt_keys, "prompt_values": prompt_values, "suffix_keys": suffix_keys, "suffix_values": suffix_values, "new_keys": new_keys, "new_values": new_values, "out_weight": out_weight, "span_perm": span_perm, "share_counts": share_counts, "sample_perm": sample_perm, "decoded_lens": decoded_lens}


lowest = -1.0e30


def rounded(values):
    return lax.optimization_barrier(values.astype(jnp.bfloat16)).astype(jnp.float32)


def reference(queries, prompt_keys, prompt_values, suffix_keys, suffix_values, new_keys, new_values, out_weight, span_perm, share_counts, sample_perm, decoded_lens):
    grouped = H // KVH
    scaling = 1.0 / (HD ** 0.5)
    inverse = jnp.zeros((SPANS,), jnp.int32).at[span_perm].set(jnp.arange(SPANS, dtype=jnp.int32))
    sorted_keys = prompt_keys.reshape(SPANS, SPAN, KVH, HD)[inverse].reshape(PROMPTS, PLEN, KVH, HD)
    sorted_values = prompt_values.reshape(SPANS, SPAN, KVH, HD)[inverse].reshape(PROMPTS, PLEN, KVH, HD)
    prompt_ends = jnp.cumsum(share_counts).astype(jnp.int32)
    prompt_of = jnp.sum((sample_perm[:, None] >= prompt_ends[None, :]).astype(jnp.int32), axis=1).astype(jnp.int32)
    query_rows = queries.reshape(SAMPLES, 3, KVH, grouped, HD)
    suffix_key_rows = suffix_keys.reshape(SAMPLES, SUF, KVH, HD)
    suffix_value_rows = suffix_values.reshape(SAMPLES, SUF, KVH, HD)
    fresh_key_rows = new_keys.reshape(SAMPLES, 3, KVH, HD)
    fresh_value_rows = new_values.reshape(SAMPLES, 3, KVH, HD)
    causal = jnp.arange(3)[None, :] <= jnp.arange(3)[:, None]
    positions = jnp.arange(SUF)

    def attend_sample(sample):
        prompt = prompt_of[sample]
        own_query = query_rows[sample].astype(jnp.float32)
        prompt_scores = jnp.einsum("jkgd,tkd->jkgt", own_query, sorted_keys[prompt].astype(jnp.float32)) * scaling
        suffix_scores = jnp.einsum("jkgd,tkd->jkgt", own_query, suffix_key_rows[sample].astype(jnp.float32)) * scaling
        fresh_scores = jnp.einsum("jkgd,tkd->jkgt", own_query, fresh_key_rows[sample].astype(jnp.float32)) * scaling
        suffix_mask = (positions < decoded_lens[sample])[None, None, None, :]
        fresh_mask = causal[:, None, None, :]
        row_max = jnp.maximum(
            jnp.max(prompt_scores, axis=-1),
            jnp.maximum(
                jnp.max(jnp.where(suffix_mask, suffix_scores, lowest), axis=-1),
                jnp.max(jnp.where(fresh_mask, fresh_scores, lowest), axis=-1),
            ),
        )
        prompt_weights = rounded(jnp.exp(prompt_scores - row_max[..., None]))
        suffix_weights = rounded(jnp.where(suffix_mask, jnp.exp(suffix_scores - row_max[..., None]), 0.0))
        fresh_weights = rounded(jnp.where(fresh_mask, jnp.exp(fresh_scores - row_max[..., None]), 0.0))
        total = jnp.sum(prompt_weights, axis=-1) + jnp.sum(suffix_weights, axis=-1) + jnp.sum(fresh_weights, axis=-1)
        output = jnp.einsum("jkgt,tkd->jkgd", prompt_weights, sorted_values[prompt].astype(jnp.float32))
        output = output + jnp.einsum("jkgt,tkd->jkgd", suffix_weights, suffix_value_rows[sample].astype(jnp.float32))
        output = output + jnp.einsum("jkgt,tkd->jkgd", fresh_weights, fresh_value_rows[sample].astype(jnp.float32))
        return (output / total[..., None]).astype(jnp.bfloat16).reshape(3, H * HD)

    attended = lax.map(attend_sample, jnp.arange(SAMPLES, dtype=jnp.int32)).reshape(SAMPLES * 3, H * HD)
    return jnp.dot(attended, out_weight, preferred_element_type=jnp.float32)
```

```python
import functools
import math

import jax
import jax.numpy as jnp
from jax import lax
from jax.experimental import pallas as pl
from jax.experimental.pallas import tpu as pltpu
from jax.sharding import PartitionSpec as P

H = 64
KVH = 8
HD = 128
PLEN = 8192
SPAN = 256
SUF = 256
NZ = 8
NX = 4
TASKS = NZ * NX
SHARD = 768
OWN = 32
CHUNK = 16
ROWS = CHUNK * 24
SLOTS = 16
GROUPS = SHARD // 128
LOWEST = -1.0e30
MESH_ID = pl.DeviceIdType.MESH
F32 = jnp.float32
BF16 = jnp.bfloat16
LOG2E = math.log2(math.e)
SCALE = 1.0 / math.sqrt(HD)
XROWS = 256


class Hop:
    def __init__(self, index, axis, way, dz, dx, low, high, deps):
        self.index, self.axis, self.way = index, axis, way
        self.dz, self.dx, self.low, self.high, self.deps = dz, dx, low, high, deps
        self.kids = []


def gather_tree():
    hops = []

    def add(axis, way, dz, dx, rows, deps):
        hop = Hop(len(hops), axis, way, dz, dx, rows[0], rows[1], deps)
        hops.append(hop)
        return hop

    def ring(axis, size, rows, base, dz, dx):
        middle = (rows[0] + rows[1]) // 2
        held = {0: base}
        far = size // 2
        for way in (1, -1):
            deps = base
            for step in range(1, far):
                place = (step * way, dx) if axis == "z" else (dz, step * way)
                deps = [add(axis, way, place[0], place[1], rows, deps)]
                held[step * way] = deps
            half = (rows[0], middle) if way == 1 else (middle, rows[1])
            place = (far, dx) if axis == "z" else (dz, far)
            held.setdefault(far, []).append(add(axis, way, place[0], place[1], half, deps))
        return held

    rows_x, rows_z = (0, XROWS), (XROWS, SHARD)
    for dx, base in ring("x", NX, rows_x, [], 0, 0).items():
        ring("z", NZ, rows_x, base, 0, dx)
    for dz, base in ring("z", NZ, rows_z, [], 0, 0).items():
        ring("x", NX, rows_z, base, dz, 0)
    for hop in hops:
        for dep in hop.deps:
            dep.kids.append(hop)
    free, arrival = {}, {}
    pending = [(0.0, hop.index) for hop in hops if not hop.deps]
    while pending:
        pending.sort()
        ready, index = pending.pop(0)
        hop = hops[index]
        link = (hop.axis, hop.way)
        start = max(ready, free.get(link, 0.0))
        free[link] = start + (hop.high - hop.low) * 256 * 2 / 90e3
        arrival[index] = free[link] + 1.0
        for kid in hop.kids:
            if all(dep.index in arrival for dep in kid.deps):
                pending.append((max(arrival[dep.index] for dep in kid.deps), kid.index))
    return sorted(hops, key=lambda hop: arrival[hop.index])


TREE = gather_tree()


def place():
    task = lax.axis_index("task")
    return task // NX, lax.rem(task, NX)


def task_at(z, x):
    return lax.rem(z + 2 * NZ, NZ) * NX + lax.rem(x + 2 * NX, NX)


def greet_neighbours(z, x):
    barrier = pltpu.get_barrier_semaphore()
    for dz, dx in ((1, 0), (-1, 0), (0, 1), (0, -1)):
        pl.semaphore_signal(
            barrier, inc=1, device_id={"task": task_at(z + dz, x + dx)}, device_id_type=MESH_ID
        )
    pl.semaphore_wait(barrier, 4)


def suffix_pair(pair, q_ref, sk_ref, sv_ref, nk_ref, nv_ref, lens_ref, o_ref, lam_ref):
    q = q_ref[pl.ds(48 * pair, 48), :]
    row = lax.broadcasted_iota(jnp.int32, (48, SUF), 0)
    col = lax.broadcasted_iota(jnp.int32, (48, SUF), 1)
    first = row < 24
    nt = (((1,), (1,)), ((), ()))
    k0 = sk_ref[pl.ds(512 * pair, SUF), :]
    k1 = sk_ref[pl.ds(512 * pair + SUF, SUF), :]
    s0 = lax.dot_general(q, k0, nt, preferred_element_type=F32)
    s1 = lax.dot_general(q, k1, nt, preferred_element_type=F32)
    length = jnp.where(first, lens_ref[2 * pair], lens_ref[2 * pair + 1])
    s = jnp.where(col < length, jnp.where(first, s0, s1) * SCALE, LOWEST)
    f = lax.dot_general(q, nk_ref[...], nt, preferred_element_type=F32) * SCALE
    frow = lax.broadcasted_iota(jnp.int32, (48, 96), 0)
    fcol = lax.broadcasted_iota(jnp.int32, (48, 96), 1)
    later = jnp.where(frow < 24, 0, 1)
    position = (frow - 24 * later) >> 3
    ahead = fcol - 3 * (2 * pair + later)
    f = jnp.where((ahead >= 0) & (ahead <= position), f, LOWEST)
    top = jnp.maximum(jnp.max(s, axis=-1, keepdims=True), jnp.max(f, axis=-1, keepdims=True))
    ws = jnp.exp(s - top)
    wf = jnp.exp(f - top).astype(BF16)
    w0 = jnp.where(first, ws, 0.0).astype(BF16)
    w1 = jnp.where(first, 0.0, ws).astype(BF16)
    total = jnp.sum(w0.astype(F32) + w1.astype(F32), axis=-1, keepdims=True) + jnp.sum(
        wf.astype(F32), axis=-1, keepdims=True
    )
    out = jnp.dot(w0, sv_ref[pl.ds(512 * pair, SUF), :], preferred_element_type=F32)
    out = out + jnp.dot(w1, sv_ref[pl.ds(512 * pair + SUF, SUF), :], preferred_element_type=F32)
    out = out + jnp.dot(wf, nv_ref[...], preferred_element_type=F32)
    o_ref[pl.ds(48 * pair, 48), :] = out / total
    lam_ref[pl.ds(48 * pair, 48), :] = jnp.broadcast_to(top + jnp.log(total), (48, 128))


def gather_kernel(
    q_ref, sk_ref, sv_ref, nk_ref, nv_ref, lens_ref, all_ref, o_ref, lam_ref,
    wide_ref, own_sem, send_sems, recv_sems,
):
    z, x = place()
    greet_neighbours(z, x)
    own = pltpu.make_async_copy(q_ref, all_ref.at[task_at(z, x)], own_sem)
    own.start()

    def copy(hop):
        sz, sx = (hop.way, 0) if hop.axis == "z" else (0, hop.way)
        origin = task_at(z - hop.dz + sz, x - hop.dx + sx)
        rows = pl.ds(hop.low, hop.high - hop.low)
        target = all_ref.at[origin, rows]
        return pltpu.make_async_remote_copy(
            src_ref=q_ref.at[rows] if not hop.deps else target,
            dst_ref=target,
            send_sem=send_sems.at[hop.index],
            recv_sem=recv_sems.at[hop.index],
            device_id={"task": task_at(z + sz, x + sx)},
            device_id_type=MESH_ID,
        )

    for hop in TREE:
        if not hop.deps:
            copy(hop).start()
    done = set()
    pair = 0
    for count, hop in enumerate(TREE):
        if count % 4 == 0 and pair < OWN // 2:
            suffix_pair(pair, q_ref, sk_ref, sv_ref, nk_ref, nv_ref, lens_ref, o_ref, wide_ref)
            pair += 1
        copy(hop).wait_recv()
        done.add(hop.index)
        for kid in hop.kids:
            if all(dep.index in done for dep in kid.deps):
                copy(kid).start()
    for g in range(GROUPS):
        lam_ref[g] = jnp.transpose(wide_ref[pl.ds(128 * g, 128), :])[0:1, :]
    own.wait()
    for hop in TREE:
        copy(hop).wait_send()


VMEM_SPEC = pl.BlockSpec(memory_space=pltpu.VMEM)
SMEM_SPEC = pl.BlockSpec(memory_space=pltpu.SMEM)
ANY_SPEC = pl.BlockSpec(memory_space=pl.ANY)


def gather_queries(q, suffix_keys, suffix_values, new_keys, new_values, lens):
    hops = len(TREE)
    return pl.pallas_call(
        gather_kernel,
        out_shape=(
            jax.ShapeDtypeStruct((TASKS, SHARD, HD), BF16),
            jax.ShapeDtypeStruct((SHARD, HD), F32),
            jax.ShapeDtypeStruct((GROUPS, 1, 128), F32),
        ),
        in_specs=[VMEM_SPEC] * 5 + [SMEM_SPEC],
        out_specs=(ANY_SPEC, VMEM_SPEC, VMEM_SPEC),
        scratch_shapes=[
            pltpu.VMEM((SHARD, 128), F32),
            pltpu.SemaphoreType.DMA,
            pltpu.SemaphoreType.DMA((hops,)),
            pltpu.SemaphoreType.DMA((hops,)),
        ],
        compiler_params=pltpu.CompilerParams(
            collective_id=0, has_side_effects=True, vmem_limit_bytes=48 * 2**20
        ),
        name="gather_queries",
    )(q, suffix_keys, suffix_values, new_keys, new_values, lens)


def prompt_kernel(
    order_ref, counts_ref, span_ref, q_ref, k_ref, v_ref, out_ref, lam_ref,
    o_ref, wide_ref, qs_ref, acc_ref, top_ref, blocks_ref, have_ref,
):
    for p in range(16):
        have_ref[p] = 0
    for slot in range(SLOTS):
        p = span_ref[slot] >> 5
        blocks_ref[p * SLOTS + have_ref[p]] = slot
        have_ref[p] = have_ref[p] + 1

    ones = jnp.ones((SPAN, 128), BF16)
    nt = (((1,), (1,)), ((), ()))

    def fill(first, count):
        def one(i, carry):
            at = pl.multiple_of(order_ref[first + i] * 24, 8)
            o_ref[pl.ds(at, 24), :] = jnp.zeros((24, 128), F32)
            wide_ref[pl.ds(at, 24), :] = jnp.full((24, 128), LOWEST, F32)
            return carry

        lax.fori_loop(0, count, one, 0)

    def attend(p, first, count):
        have = have_ref[p]

        def chunk(c, carry):
            base = first + c * CHUNK
            samples = [order_ref[jnp.minimum(base + i, first + count - 1)] for i in range(CHUNK)]
            for i, s in enumerate(samples):
                at = pl.multiple_of((s >> 1) * 48, 16)
                both = q_ref[pl.ds(at, 48), :].astype(F32)
                qs_ref[pl.ds(24 * i, 24), :] = jnp.where((s & 1) == 1, both[24:48], both[0:24])
            top_ref[...] = jnp.full((ROWS, 128), LOWEST, F32)
            acc_ref[...] = jnp.zeros((ROWS, 256), F32)

            def block(b, inner):
                slot = blocks_ref[p * SLOTS + b]
                at = pl.multiple_of(slot * SPAN, SPAN)
                keys = k_ref[pl.ds(at, SPAN), :]
                values = jnp.concatenate([v_ref[pl.ds(at, SPAN), :], ones], axis=1)
                for part in range(3):
                    rows = pl.ds(128 * part, 128)
                    q = qs_ref[rows, :].astype(BF16)
                    s = lax.dot_general(q, keys, nt, preferred_element_type=F32) * (SCALE * LOG2E)
                    old = top_ref[rows, :]
                    new = jnp.maximum(old, jnp.max(s, axis=-1, keepdims=True))
                    w = jnp.exp2(s - jnp.concatenate([new, new], axis=1)).astype(BF16)
                    decay = jnp.exp2(old - new)
                    acc_ref[rows, :] = acc_ref[rows, :] * jnp.concatenate(
                        [decay, decay], axis=1
                    ) + jnp.dot(w, values, preferred_element_type=F32)
                    top_ref[rows, :] = new
                return inner

            lax.fori_loop(0, have, block, 0)
            for i, s in enumerate(samples):
                rows = pl.ds(24 * i, 24)
                total = acc_ref[rows, pl.ds(128, 128)]
                at = pl.multiple_of(s * 24, 8)
                o_ref[pl.ds(at, 24), :] = acc_ref[rows, pl.ds(0, 128)] / total
                wide_ref[pl.ds(at, 24), :] = top_ref[rows, :] * (1.0 / LOG2E) + jnp.log(total)
            return carry

        lax.fori_loop(0, (count + CHUNK - 1) // CHUNK, chunk, 0)

    def prompt(p, first):
        count = counts_ref[p]

        @pl.when(have_ref[p] == 0)
        def _():
            fill(first, count)

        @pl.when(have_ref[p] > 0)
        def _():
            attend(p, first, count)

        return first + count

    lax.fori_loop(0, 16, prompt, 0)

    def finish(t, carry):
        at = pl.multiple_of(t * SHARD, SHARD)
        out_ref[pl.ds(at, SHARD), :] = o_ref[pl.ds(at, SHARD), :].astype(BF16)
        eye = lax.broadcasted_iota(jnp.int32, (128, 128), 0) == lax.broadcasted_iota(
            jnp.int32, (128, 128), 1
        )
        for g in range(GROUPS):
            tile = wide_ref[pl.ds(pl.multiple_of(at + 128 * g, 128), 128), :]
            lam_ref[t * GROUPS + g] = jnp.sum(jnp.where(eye, tile, 0.0), axis=0, keepdims=True)
        return carry

    lax.fori_loop(0, TASKS, finish, 0)


def attend_prompts(order, counts, spans, q_all, keys, values):
    rows = TASKS * SHARD
    return pl.pallas_call(
        prompt_kernel,
        out_shape=(
            jax.ShapeDtypeStruct((rows, HD), BF16),
            jax.ShapeDtypeStruct((TASKS * GROUPS, 1, 128), F32),
        ),
        in_specs=[SMEM_SPEC] * 3 + [VMEM_SPEC] * 3,
        out_specs=(VMEM_SPEC, VMEM_SPEC),
        scratch_shapes=[
            pltpu.VMEM((rows, 128), F32),
            pltpu.VMEM((rows, 128), F32),
            pltpu.VMEM((ROWS, 128), F32),
            pltpu.VMEM((ROWS, 256), F32),
            pltpu.VMEM((ROWS, 128), F32),
            pltpu.SMEM((16 * SLOTS,), jnp.int32),
            pltpu.SMEM((16,), jnp.int32),
        ],
        compiler_params=pltpu.CompilerParams(vmem_limit_bytes=56 * 2**20),
        name="attend_prompts",
    )(order, counts, spans, q_all.reshape(rows, HD), keys, values)


def merge_kernel(
    part_in, lam_in, own_ref, own_lam_ref, out_ref,
    part_ref, lam_ref, land_ref, lland_ref, in_sem, send_sems, recv_sems, lsend_sems, lrecv_sems,
):
    z, x = place()
    load = pltpu.make_async_copy(part_in, part_ref, in_sem.at[0])
    lload = pltpu.make_async_copy(lam_in, lam_ref, in_sem.at[1])
    load.start()
    lload.start()
    greet_neighbours(z, x)
    load.wait()
    lload.wait()
    offsets, at = {}, 0
    for hop in TREE:
        offsets[hop.index] = at
        at += hop.high - hop.low

    def copies(hop):
        origin = task_at(z - hop.dz, x - hop.dx)
        sz, sx = (hop.way, 0) if hop.axis == "z" else (0, hop.way)
        target = {"task": task_at(z - sz, x - sx)}
        size = hop.high - hop.low
        wide = pltpu.make_async_remote_copy(
            src_ref=part_ref.at[origin, pl.ds(hop.low, size)],
            dst_ref=land_ref.at[pl.ds(offsets[hop.index], size)],
            send_sem=send_sems.at[hop.index],
            recv_sem=recv_sems.at[hop.index],
            device_id=target,
            device_id_type=MESH_ID,
        )
        thin = pltpu.make_async_remote_copy(
            src_ref=lam_ref.at[pl.ds(origin * GROUPS + hop.low // 128, size // 128)],
            dst_ref=lland_ref.at[pl.ds(offsets[hop.index] // 128, size // 128)],
            send_sem=lsend_sems.at[hop.index],
            recv_sem=lrecv_sems.at[hop.index],
            device_id=target,
            device_id_type=MESH_ID,
        )
        return thin, wide

    waited = set()

    def merge(origin, low, high, kids, last):
        for hop in kids:
            if hop.index not in waited:
                waited.add(hop.index)
                for copy in copies(hop):
                    copy.wait_recv()
        for g in range(low // 128, high // 128):
            here = [hop for hop in kids if hop.low <= 128 * g < hop.high]
            if not here and not last:
                continue
            lams = [lam_ref[origin * GROUPS + g]]
            parts = [part_ref[origin, pl.ds(128 * g, 128), :].astype(F32)]
            for hop in here:
                start = offsets[hop.index] + 128 * g - hop.low
                lams.append(lland_ref[start // 128])
                parts.append(land_ref[pl.ds(start, 128), :].astype(F32))
            if last:
                lams.append(own_lam_ref[g])
                parts.append(own_ref[pl.ds(128 * g, 128), :])
            top = functools.reduce(jnp.maximum, lams)
            shares = [jnp.exp(lam - top) for lam in lams]
            total = functools.reduce(jnp.add, shares)
            mixed = parts[0]
            for share, part in zip(shares[1:], parts[1:]):
                weight = jnp.transpose(jnp.broadcast_to(share / total, (128, 128)))
                mixed = mixed + weight * (part - parts[0])
            if last:
                out_ref[pl.ds(128 * g, 128), :] = mixed
            else:
                lam_ref[origin * GROUPS + g] = top + jnp.log(total)
                part_ref[origin, pl.ds(128 * g, 128), :] = mixed.astype(BF16)

    for hop in reversed(TREE):
        if hop.kids:
            merge(task_at(z - hop.dz, x - hop.dx), hop.low, hop.high, hop.kids, False)
        for copy in copies(hop):
            copy.start()
    merge(task_at(z, x), 0, SHARD, [hop for hop in TREE if not hop.deps], True)
    for hop in TREE:
        for copy in copies(hop):
            copy.wait_send()


def merge_parts(parts, lams, own, own_lam):
    hops = len(TREE)
    landed = sum(hop.high - hop.low for hop in TREE)
    return pl.pallas_call(
        merge_kernel,
        out_shape=jax.ShapeDtypeStruct((SHARD, HD), F32),
        in_specs=[ANY_SPEC, ANY_SPEC, VMEM_SPEC, VMEM_SPEC],
        out_specs=VMEM_SPEC,
        scratch_shapes=[
            pltpu.VMEM((TASKS, SHARD, HD), BF16),
            pltpu.VMEM((TASKS * GROUPS, 1, 128), F32),
            pltpu.VMEM((landed, HD), BF16),
            pltpu.VMEM((landed // 128, 1, 128), F32),
            pltpu.SemaphoreType.DMA((2,)),
            pltpu.SemaphoreType.DMA((hops,)),
            pltpu.SemaphoreType.DMA((hops,)),
            pltpu.SemaphoreType.DMA((hops,)),
            pltpu.SemaphoreType.DMA((hops,)),
        ],
        compiler_params=pltpu.CompilerParams(
            collective_id=1, has_side_effects=True, vmem_limit_bytes=48 * 2**20
        ),
        name="merge_parts",
    )(parts.reshape(TASKS, SHARD, HD), lams, own, own_lam)


def on_device(
    queries, prompt_keys, prompt_values, suffix_keys, suffix_values, new_keys, new_values,
    out_weight, span_perm, share_counts, sample_perm, decoded_lens,
):
    samples = sample_perm.shape[0]
    ids = jnp.arange(samples, dtype=jnp.int32)
    order = jnp.sum(jnp.where(sample_perm[None, :] == ids[:, None], ids[None, :], 0), axis=1)
    q = queries.reshape(SHARD, HD)
    q_all, own, own_lam = gather_queries(
        q, suffix_keys, suffix_values, new_keys, new_values, decoded_lens
    )
    parts, lams = attend_prompts(order, share_counts, span_perm, q_all, prompt_keys, prompt_values)
    attended = merge_parts(parts, lams, own, own_lam).astype(BF16).reshape(OWN * 3, 8 * HD)
    every_row = lax.all_gather(attended, "task", axis=0, tiled=True)
    return lax.psum_scatter(
        jnp.dot(every_row, out_weight, preferred_element_type=F32),
        "tp",
        scatter_dimension=0,
        tiled=True,
    )


def solution(mesh):
    return jax.shard_map(
        on_device,
        mesh=mesh,
        in_specs=(
            P("task", "tp"), P("task", "tp"), P("task", "tp"), P("task", "tp"), P("task", "tp"),
            P("task", "tp"), P("task", "tp"), P("tp", "task"), P("task"), P(), P(), P("task"),
        ),
        out_specs=P("tp", "task"),
        check_vma=False,
    )
```

```python
import functools
import math

import jax
import jax.numpy as jnp
from jax import lax
from jax.experimental import pallas as pl
from jax.experimental.pallas import tpu as pltpu
from jax.sharding import PartitionSpec as P

H = 64
KVH = 8
HD = 128
PLEN = 8192
SPAN = 256
SUF = 256
NZ = 8
NX = 4
TASKS = NZ * NX
SHARD = 768
OWN = 32
CHUNK = 16
ROWS = CHUNK * 24
SLOTS = 16
GROUPS = SHARD // 128
LOWEST = -1.0e30
MESH_ID = pl.DeviceIdType.MESH
F32 = jnp.float32
BF16 = jnp.bfloat16
LOG2E = math.log2(math.e)
SCALE = 1.0 / math.sqrt(HD)
XROWS = 256


class Hop:
    def __init__(self, index, axis, way, dz, dx, low, high, deps):
        self.index, self.axis, self.way = index, axis, way
        self.dz, self.dx, self.low, self.high, self.deps = dz, dx, low, high, deps
        self.kids = []


def gather_tree():
    hops = []

    def add(axis, way, dz, dx, rows, deps):
        hop = Hop(len(hops), axis, way, dz, dx, rows[0], rows[1], deps)
        hops.append(hop)
        return hop

    def ring(axis, size, rows, base, dz, dx):
        middle = (rows[0] + rows[1]) // 2
        held = {0: base}
        far = size // 2
        for way in (1, -1):
            deps = base
            for step in range(1, far):
                place = (step * way, dx) if axis == "z" else (dz, step * way)
                deps = [add(axis, way, place[0], place[1], rows, deps)]
                held[step * way] = deps
            half = (rows[0], middle) if way == 1 else (middle, rows[1])
            place = (far, dx) if axis == "z" else (dz, far)
            held.setdefault(far, []).append(add(axis, way, place[0], place[1], half, deps))
        return held

    rows_x, rows_z = (0, XROWS), (XROWS, SHARD)
    for dx, base in ring("x", NX, rows_x, [], 0, 0).items():
        ring("z", NZ, rows_x, base, 0, dx)
    for dz, base in ring("z", NZ, rows_z, [], 0, 0).items():
        ring("x", NX, rows_z, base, dz, 0)
    for hop in hops:
        for dep in hop.deps:
            dep.kids.append(hop)
    free, arrival = {}, {}
    pending = [(0.0, hop.index) for hop in hops if not hop.deps]
    while pending:
        pending.sort()
        ready, index = pending.pop(0)
        hop = hops[index]
        link = (hop.axis, hop.way)
        start = max(ready, free.get(link, 0.0))
        free[link] = start + (hop.high - hop.low) * 256 * 2 / 90e3
        arrival[index] = free[link] + 1.0
        for kid in hop.kids:
            if all(dep.index in arrival for dep in kid.deps):
                pending.append((max(arrival[dep.index] for dep in kid.deps), kid.index))
    return sorted(hops, key=lambda hop: arrival[hop.index])


TREE = gather_tree()


def place():
    task = lax.axis_index("task")
    return task // NX, lax.rem(task, NX)


def task_at(z, x):
    return lax.rem(z + 2 * NZ, NZ) * NX + lax.rem(x + 2 * NX, NX)


def greet(devices):
    barrier = pltpu.get_barrier_semaphore()
    for device in devices:
        pl.semaphore_signal(barrier, inc=1, device_id=device, device_id_type=MESH_ID)
    pl.semaphore_wait(barrier, len(devices))


def plane_neighbours(z, x):
    return [{"task": task_at(z + dz, x + dx)} for dz, dx in ((1, 0), (-1, 0), (0, 1), (0, -1))]


def suffix_pair(pair, q_ref, sk_ref, sv_ref, nk_ref, nv_ref, lens_ref, o_ref, lam_ref):
    q = q_ref[pl.ds(48 * pair, 48), :]
    row = lax.broadcasted_iota(jnp.int32, (48, SUF), 0)
    col = lax.broadcasted_iota(jnp.int32, (48, SUF), 1)
    first = row < 24
    nt = (((1,), (1,)), ((), ()))
    k0 = sk_ref[pl.ds(512 * pair, SUF), :]
    k1 = sk_ref[pl.ds(512 * pair + SUF, SUF), :]
    s0 = lax.dot_general(q, k0, nt, preferred_element_type=F32)
    s1 = lax.dot_general(q, k1, nt, preferred_element_type=F32)
    length = jnp.where(first, lens_ref[2 * pair], lens_ref[2 * pair + 1])
    s = jnp.where(col < length, jnp.where(first, s0, s1) * SCALE, LOWEST)
    f = lax.dot_general(q, nk_ref[...], nt, preferred_element_type=F32) * SCALE
    frow = lax.broadcasted_iota(jnp.int32, (48, 96), 0)
    fcol = lax.broadcasted_iota(jnp.int32, (48, 96), 1)
    later = jnp.where(frow < 24, 0, 1)
    position = (frow - 24 * later) >> 3
    ahead = fcol - 3 * (2 * pair + later)
    f = jnp.where((ahead >= 0) & (ahead <= position), f, LOWEST)
    top = jnp.maximum(jnp.max(s, axis=-1, keepdims=True), jnp.max(f, axis=-1, keepdims=True))
    ws = jnp.exp(s - top)
    wf = jnp.exp(f - top).astype(BF16)
    w0 = jnp.where(first, ws, 0.0).astype(BF16)
    w1 = jnp.where(first, 0.0, ws).astype(BF16)
    total = jnp.sum(w0.astype(F32) + w1.astype(F32), axis=-1, keepdims=True) + jnp.sum(
        wf.astype(F32), axis=-1, keepdims=True
    )
    out = jnp.dot(w0, sv_ref[pl.ds(512 * pair, SUF), :], preferred_element_type=F32)
    out = out + jnp.dot(w1, sv_ref[pl.ds(512 * pair + SUF, SUF), :], preferred_element_type=F32)
    out = out + jnp.dot(wf, nv_ref[...], preferred_element_type=F32)
    o_ref[pl.ds(48 * pair, 48), :] = out / total
    lam_ref[pl.ds(48 * pair, 48), :] = jnp.broadcast_to(top + jnp.log(total), (48, 128))


def gather_kernel(
    q_ref, sk_ref, sv_ref, nk_ref, nv_ref, lens_ref, all_ref, o_ref, lam_ref,
    wide_ref, own_sem, send_sems, recv_sems,
):
    z, x = place()
    greet(plane_neighbours(z, x))
    own = pltpu.make_async_copy(q_ref, all_ref.at[task_at(z, x)], own_sem)
    own.start()

    def copy(hop):
        sz, sx = (hop.way, 0) if hop.axis == "z" else (0, hop.way)
        origin = task_at(z - hop.dz + sz, x - hop.dx + sx)
        rows = pl.ds(hop.low, hop.high - hop.low)
        target = all_ref.at[origin, rows]
        return pltpu.make_async_remote_copy(
            src_ref=q_ref.at[rows] if not hop.deps else target,
            dst_ref=target,
            send_sem=send_sems.at[hop.index],
            recv_sem=recv_sems.at[hop.index],
            device_id={"task": task_at(z + sz, x + sx)},
            device_id_type=MESH_ID,
        )

    for hop in TREE:
        if not hop.deps:
            copy(hop).start()
    done = set()
    pair = 0
    for count, hop in enumerate(TREE):
        if count % 4 == 0 and pair < OWN // 2:
            suffix_pair(pair, q_ref, sk_ref, sv_ref, nk_ref, nv_ref, lens_ref, o_ref, wide_ref)
            pair += 1
        copy(hop).wait_recv()
        done.add(hop.index)
        for kid in hop.kids:
            if all(dep.index in done for dep in kid.deps):
                copy(kid).start()
    for g in range(GROUPS):
        lam_ref[g] = jnp.transpose(wide_ref[pl.ds(128 * g, 128), :])[0:1, :]
    own.wait()
    for hop in TREE:
        copy(hop).wait_send()


VMEM_SPEC = pl.BlockSpec(memory_space=pltpu.VMEM)
SMEM_SPEC = pl.BlockSpec(memory_space=pltpu.SMEM)
ANY_SPEC = pl.BlockSpec(memory_space=pl.ANY)


def gather_queries(q, suffix_keys, suffix_values, new_keys, new_values, lens):
    hops = len(TREE)
    return pl.pallas_call(
        gather_kernel,
        out_shape=(
            jax.ShapeDtypeStruct((TASKS, SHARD, HD), BF16),
            jax.ShapeDtypeStruct((SHARD, HD), F32),
            jax.ShapeDtypeStruct((GROUPS, 1, 128), F32),
        ),
        in_specs=[VMEM_SPEC] * 5 + [SMEM_SPEC],
        out_specs=(ANY_SPEC, VMEM_SPEC, VMEM_SPEC),
        scratch_shapes=[
            pltpu.VMEM((SHARD, 128), F32),
            pltpu.SemaphoreType.DMA,
            pltpu.SemaphoreType.DMA((hops,)),
            pltpu.SemaphoreType.DMA((hops,)),
        ],
        compiler_params=pltpu.CompilerParams(
            collective_id=0, has_side_effects=True, vmem_limit_bytes=48 * 2**20
        ),
        name="gather_queries",
    )(q, suffix_keys, suffix_values, new_keys, new_values, lens)


def prompt_kernel(
    order_ref, counts_ref, span_ref, q_ref, k_ref, v_ref, out_ref, lam_ref,
    o_ref, wide_ref, qs_ref, acc_ref, top_ref, blocks_ref, have_ref,
):
    for p in range(16):
        have_ref[p] = 0
    for slot in range(SLOTS):
        p = span_ref[slot] >> 5
        blocks_ref[p * SLOTS + have_ref[p]] = slot
        have_ref[p] = have_ref[p] + 1

    ones = jnp.ones((SPAN, 128), BF16)
    nt = (((1,), (1,)), ((), ()))

    def fill(first, count):
        def one(i, carry):
            at = pl.multiple_of(order_ref[first + i] * 24, 8)
            o_ref[pl.ds(at, 24), :] = jnp.zeros((24, 128), F32)
            wide_ref[pl.ds(at, 24), :] = jnp.full((24, 128), LOWEST, F32)
            return carry

        lax.fori_loop(0, count, one, 0)

    def attend(p, first, count):
        have = have_ref[p]

        def chunk(c, carry):
            base = first + c * CHUNK
            samples = [order_ref[jnp.minimum(base + i, first + count - 1)] for i in range(CHUNK)]
            for i, s in enumerate(samples):
                at = pl.multiple_of((s >> 1) * 48, 16)
                both = q_ref[pl.ds(at, 48), :].astype(F32)
                qs_ref[pl.ds(24 * i, 24), :] = jnp.where((s & 1) == 1, both[24:48], both[0:24])
            top_ref[...] = jnp.full((ROWS, 128), LOWEST, F32)
            acc_ref[...] = jnp.zeros((ROWS, 256), F32)

            def block(b, inner):
                slot = blocks_ref[p * SLOTS + b]
                at = pl.multiple_of(slot * SPAN, SPAN)
                keys = k_ref[pl.ds(at, SPAN), :]
                values = jnp.concatenate([v_ref[pl.ds(at, SPAN), :], ones], axis=1)
                for part in range(3):
                    rows = pl.ds(128 * part, 128)
                    q = qs_ref[rows, :].astype(BF16)
                    s = lax.dot_general(q, keys, nt, preferred_element_type=F32) * (SCALE * LOG2E)
                    old = top_ref[rows, :]
                    new = jnp.maximum(old, jnp.max(s, axis=-1, keepdims=True))
                    w = jnp.exp2(s - jnp.concatenate([new, new], axis=1)).astype(BF16)
                    decay = jnp.exp2(old - new)
                    acc_ref[rows, :] = acc_ref[rows, :] * jnp.concatenate(
                        [decay, decay], axis=1
                    ) + jnp.dot(w, values, preferred_element_type=F32)
                    top_ref[rows, :] = new
                return inner

            lax.fori_loop(0, have, block, 0)
            for i, s in enumerate(samples):
                rows = pl.ds(24 * i, 24)
                total = acc_ref[rows, pl.ds(128, 128)]
                at = pl.multiple_of(s * 24, 8)
                o_ref[pl.ds(at, 24), :] = acc_ref[rows, pl.ds(0, 128)] / total
                wide_ref[pl.ds(at, 24), :] = top_ref[rows, :] * (1.0 / LOG2E) + jnp.log(total)
            return carry

        lax.fori_loop(0, (count + CHUNK - 1) // CHUNK, chunk, 0)

    def prompt(p, first):
        count = counts_ref[p]

        @pl.when(have_ref[p] == 0)
        def _():
            fill(first, count)

        @pl.when(have_ref[p] > 0)
        def _():
            attend(p, first, count)

        return first + count

    lax.fori_loop(0, 16, prompt, 0)

    def finish(t, carry):
        at = pl.multiple_of(t * SHARD, SHARD)
        out_ref[pl.ds(at, SHARD), :] = o_ref[pl.ds(at, SHARD), :].astype(BF16)
        eye = lax.broadcasted_iota(jnp.int32, (128, 128), 0) == lax.broadcasted_iota(
            jnp.int32, (128, 128), 1
        )
        for g in range(GROUPS):
            tile = wide_ref[pl.ds(pl.multiple_of(at + 128 * g, 128), 128), :]
            lam_ref[t * GROUPS + g] = jnp.sum(jnp.where(eye, tile, 0.0), axis=0, keepdims=True)
        return carry

    lax.fori_loop(0, TASKS, finish, 0)


def attend_prompts(order, counts, spans, q_all, keys, values):
    rows = TASKS * SHARD
    return pl.pallas_call(
        prompt_kernel,
        out_shape=(
            jax.ShapeDtypeStruct((rows, HD), BF16),
            jax.ShapeDtypeStruct((TASKS * GROUPS, 1, 128), F32),
        ),
        in_specs=[SMEM_SPEC] * 3 + [VMEM_SPEC] * 3,
        out_specs=(VMEM_SPEC, VMEM_SPEC),
        scratch_shapes=[
            pltpu.VMEM((rows, 128), F32),
            pltpu.VMEM((rows, 128), F32),
            pltpu.VMEM((ROWS, 128), F32),
            pltpu.VMEM((ROWS, 256), F32),
            pltpu.VMEM((ROWS, 128), F32),
            pltpu.SMEM((16 * SLOTS,), jnp.int32),
            pltpu.SMEM((16,), jnp.int32),
        ],
        compiler_params=pltpu.CompilerParams(vmem_limit_bytes=56 * 2**20),
        name="attend_prompts",
    )(order, counts, spans, q_all.reshape(rows, HD), keys, values)


def merge_kernel(
    part_in, lam_in, own_ref, own_lam_ref, w_ref, out_ref,
    part_ref, lam_ref, land_ref, lland_ref, mix_ref, a_ref, p_ref, c_ref, y_ref, yland_ref, r_ref,
    in_sem, send_sems, recv_sems, lsend_sems, lrecv_sems,
    a_sems, c_sems, y_sems, x_sems,
):
    z, x = place()
    tp = lax.axis_index("tp")
    y, core = tp // 2, lax.rem(tp, 2)
    partner = {"tp": 2 * y + 1 - core}
    up, down = ({"tp": 2 * lax.rem(y + d, 4) + core} for d in (1, 3))
    load = pltpu.make_async_copy(part_in, part_ref, in_sem.at[0])
    lload = pltpu.make_async_copy(lam_in, lam_ref, in_sem.at[1])
    load.start()
    lload.start()
    greet(plane_neighbours(z, x) + [{"task": task_at(z, x + 2)}, partner, up, down])
    load.wait()
    lload.wait()
    offsets, at = {}, 0
    for hop in TREE:
        offsets[hop.index] = at
        at += hop.high - hop.low

    def copies(hop):
        origin = task_at(z - hop.dz, x - hop.dx)
        sz, sx = (hop.way, 0) if hop.axis == "z" else (0, hop.way)
        target = {"task": task_at(z - sz, x - sx)}
        size = hop.high - hop.low
        wide = pltpu.make_async_remote_copy(
            src_ref=part_ref.at[origin, pl.ds(hop.low, size)],
            dst_ref=land_ref.at[pl.ds(offsets[hop.index], size)],
            send_sem=send_sems.at[hop.index],
            recv_sem=recv_sems.at[hop.index],
            device_id=target,
            device_id_type=MESH_ID,
        )
        thin = pltpu.make_async_remote_copy(
            src_ref=lam_ref.at[pl.ds(origin * GROUPS + hop.low // 128, size // 128)],
            dst_ref=lland_ref.at[pl.ds(offsets[hop.index] // 128, size // 128)],
            send_sem=lsend_sems.at[hop.index],
            recv_sem=lrecv_sems.at[hop.index],
            device_id=target,
            device_id_type=MESH_ID,
        )
        return thin, wide

    waited = set()

    def merge(origin, low, high, kids, last):
        for hop in kids:
            if hop.index not in waited:
                waited.add(hop.index)
                for copy in copies(hop):
                    copy.wait_recv()
        for g in range(low // 128, high // 128):
            here = [hop for hop in kids if hop.low <= 128 * g < hop.high]
            if not here and not last:
                continue
            lams = [lam_ref[origin * GROUPS + g]]
            parts = [part_ref[origin, pl.ds(128 * g, 128), :].astype(F32)]
            for hop in here:
                start = offsets[hop.index] + 128 * g - hop.low
                lams.append(lland_ref[start // 128])
                parts.append(land_ref[pl.ds(start, 128), :].astype(F32))
            if last:
                lams.append(own_lam_ref[g])
                parts.append(own_ref[pl.ds(128 * g, 128), :])
            top = functools.reduce(jnp.maximum, lams)
            shares = [jnp.exp(lam - top) for lam in lams]
            total = functools.reduce(jnp.add, shares)
            mixed = parts[0]
            for share, part in zip(shares[1:], parts[1:]):
                weight = jnp.transpose(jnp.broadcast_to(share / total, (128, 128)))
                mixed = mixed + weight * (part - parts[0])
            if last:
                mix_ref[pl.ds(128 * g, 128), :] = mixed
            else:
                lam_ref[origin * GROUPS + g] = top + jnp.log(total)
                part_ref[origin, pl.ds(128 * g, 128), :] = mixed.astype(BF16)

    for hop in reversed(TREE):
        if hop.kids:
            merge(task_at(z - hop.dz, x - hop.dx), hop.low, hop.high, hop.kids, False)
        for copy in copies(hop):
            copy.start()
    merge(task_at(z, x), 0, SHARD, [hop for hop in TREE if not hop.deps], True)
    for hop in TREE:
        for copy in copies(hop):
            copy.wait_send()

    def remote(src, dst, sems, index, device):
        return pltpu.make_async_remote_copy(
            src_ref=src, dst_ref=dst, send_sem=sems.at[0, index], recv_sem=sems.at[1, index],
            device_id=device, device_id_type=MESH_ID,
        )

    for g in range(8):
        a_ref[pl.ds(0, 96), pl.ds(128 * g, 128)] = mix_ref[
            pl.ds(g, 96, stride=8), :
        ].astype(BF16)
    slot_of = {0: 0, 1: 1, -1: 2, 2: 3, -2: 4, 3: 5, -3: 6, 4: 7, -4: 7}

    def row_copy(way, step, half):
        src = pl.ds(96 * slot_of[way * (step - 1)] + 48 * half, 48)
        dst = pl.ds(96 * slot_of[way * step] + 48 * half, 48)
        index = (step - 1) * 4 + (0 if way == 1 else 2) + half
        return remote(
            a_ref.at[src], a_ref.at[dst], a_sems, index, {"task": task_at(z + way, x)}
        )

    hops = [
        (way, step, half)
        for step in range(1, 5)
        for half in (0, 1)
        for way in (1, -1)
        if step < 4 or half == (0 if way == 1 else 1)
    ]

    def block_of(offset):
        return lax.rem(z - offset + NZ, NZ)

    def hand_over(offset):
        block = block_of(offset)
        return lax.rem(block, 2) != core, remote(
            p_ref.at[block], c_ref.at[slot_of[offset]], c_sems, slot_of[offset], partner
        )

    def project(offsets):
        first = slot_of[offsets[0]]
        rows = a_ref[pl.ds(96 * first, 96 * len(offsets)), :]
        for q in range(NX):
            product = jnp.dot(rows, w_ref[q], preferred_element_type=F32)
            for i, offset in enumerate(offsets):
                p_ref[block_of(offset), :, pl.ds(256 * q, 256)] = product[96 * i : 96 * i + 96]
        for offset in offsets:
            away, copy = hand_over(offset)

            @pl.when(away)
            def _():
                copy.start()

    def take_over(offsets):
        for offset in offsets:
            away, copy = hand_over(offset)

            @pl.when(jnp.logical_not(away))
            def _():
                copy.wait_recv()
                block = block_of(offset)
                p_ref[block] = p_ref[block] + c_ref[slot_of[offset]]

    for hop in hops:
        if hop[1] == 1:
            row_copy(*hop).start()
    turns = [[0], [1, -1], [2, -2], [3, -3], [4]]
    for step, offsets in enumerate(turns):
        for hop in hops:
            if hop[1] == step:
                row_copy(*hop).wait_recv()
                onward = (hop[0], step + 1, hop[2])
                if onward in hops:
                    row_copy(*onward).start()
        project(offsets)
        if step:
            take_over(turns[step - 1])
    take_over(turns[-1])

    def tp_block(d):
        return 2 * lax.rem(y + d, 4) + core

    top, low = pl.ds(0, 48), pl.ds(48, 48)
    far, plus, minus = tp_block(2), tp_block(1), tp_block(3)
    y_ref[0] = p_ref[far].astype(BF16)
    y_ref[1, low] = p_ref[plus, pl.ds(48, 48), :].astype(BF16)
    y_ref[2, top] = p_ref[minus, pl.ds(0, 48), :].astype(BF16)
    relay_up = remote(y_ref.at[0, top], yland_ref.at[0, top], y_sems, 0, up)
    relay_down = remote(y_ref.at[0, low], yland_ref.at[0, low], y_sems, 1, down)
    early_up = remote(y_ref.at[1, low], yland_ref.at[1, low], y_sems, 2, up)
    early_down = remote(y_ref.at[2, top], yland_ref.at[2, top], y_sems, 3, down)
    late_up = remote(y_ref.at[1, top], yland_ref.at[1, top], y_sems, 4, up)
    late_down = remote(y_ref.at[2, low], yland_ref.at[2, low], y_sems, 5, down)
    for copy in (relay_up, relay_down, early_up, early_down):
        copy.start()
    relay_up.wait_recv()
    y_ref[1, top] = (p_ref[plus, pl.ds(0, 48), :] + yland_ref[0, top].astype(F32)).astype(BF16)
    late_up.start()
    relay_down.wait_recv()
    y_ref[2, low] = (p_ref[minus, pl.ds(48, 48), :] + yland_ref[0, low].astype(F32)).astype(BF16)
    late_down.start()
    for copy in (early_up, early_down, late_up, late_down):
        copy.wait_recv()
    mine = p_ref[tp_block(0)] + yland_ref[1].astype(F32) + yland_ref[2].astype(F32)
    for q in range(NX):
        r_ref[q] = mine[:, 256 * q : 256 * q + 256]

    shares = []
    for d in (1, 2, 3):
        peer = lax.rem(x + d, NX)
        share = remote(
            r_ref.at[peer], out_ref.at[x], x_sems, d - 1, {"task": task_at(z, peer)}
        )
        share.start()
        shares.append(share)
    out_ref[x] = r_ref[x]
    for share in shares:
        share.wait_recv()
    for share in shares + [relay_up, relay_down, early_up, early_down, late_up, late_down]:
        share.wait_send()
    for hop in hops:
        row_copy(*hop).wait_send()
    for offset in slot_of:
        if offset > -4:
            away, copy = hand_over(offset)

            @pl.when(away)
            def _():
                copy.wait_send()


def merge_parts(parts, lams, own, own_lam, weights):
    hops = len(TREE)
    landed = sum(hop.high - hop.low for hop in TREE)
    return pl.pallas_call(
        merge_kernel,
        out_shape=jax.ShapeDtypeStruct((NX, 96, 256), F32),
        in_specs=[ANY_SPEC, ANY_SPEC, VMEM_SPEC, VMEM_SPEC, VMEM_SPEC],
        out_specs=VMEM_SPEC,
        scratch_shapes=[
            pltpu.VMEM((TASKS, SHARD, HD), BF16),
            pltpu.VMEM((TASKS * GROUPS, 1, 128), F32),
            pltpu.VMEM((landed, HD), BF16),
            pltpu.VMEM((landed // 128, 1, 128), F32),
            pltpu.VMEM((SHARD, HD), F32),
            pltpu.VMEM((8 * 96, 1024), BF16),
            pltpu.VMEM((8, 96, 1024), F32),
            pltpu.VMEM((8, 96, 1024), F32),
            pltpu.VMEM((3, 96, 1024), BF16),
            pltpu.VMEM((3, 96, 1024), BF16),
            pltpu.VMEM((NX, 96, 256), F32),
            pltpu.SemaphoreType.DMA((2,)),
            pltpu.SemaphoreType.DMA((hops,)),
            pltpu.SemaphoreType.DMA((hops,)),
            pltpu.SemaphoreType.DMA((hops,)),
            pltpu.SemaphoreType.DMA((hops,)),
            pltpu.SemaphoreType.DMA((2, 16)),
            pltpu.SemaphoreType.DMA((2, 8)),
            pltpu.SemaphoreType.DMA((2, 6)),
            pltpu.SemaphoreType.DMA((2, 3)),
        ],
        compiler_params=pltpu.CompilerParams(
            collective_id=1, has_side_effects=True, vmem_limit_bytes=56 * 2**20
        ),
        name="merge_parts",
    )(parts.reshape(TASKS, SHARD, HD), lams, own, own_lam, weights)


def on_device(
    queries, prompt_keys, prompt_values, suffix_keys, suffix_values, new_keys, new_values,
    out_weight, span_perm, share_counts, sample_perm, decoded_lens,
):
    samples = sample_perm.shape[0]
    ids = jnp.arange(samples, dtype=jnp.int32)
    order = jnp.sum(jnp.where(sample_perm[None, :] == ids[:, None], ids[None, :], 0), axis=1)
    q = queries.reshape(SHARD, HD)
    q_all, own, own_lam = gather_queries(
        q, suffix_keys, suffix_values, new_keys, new_values, decoded_lens
    )
    weight, q_all = lax.optimization_barrier((out_weight, q_all))
    rings = [[NX * z + x for x in range(NX)] for z in range(NZ)]
    weights = lax.all_gather(weight, "task", axis_index_groups=rings)
    parts, lams = attend_prompts(order, share_counts, span_perm, q_all, prompt_keys, prompt_values)
    return merge_parts(parts, lams, own, own_lam, weights).reshape(NX * 96, 256)


def solution(mesh):
    return jax.shard_map(
        on_device,
        mesh=mesh,
        in_specs=(
            P("task", "tp"), P("task", "tp"), P("task", "tp"), P("task", "tp"), P("task", "tp"),
            P("task", "tp"), P("task", "tp"), P("tp", "task"), P("task"), P(), P(), P("task"),
        ),
        out_specs=P("tp", "task"),
        check_vma=False,
    )
```

```python
import functools
import math

import jax
import jax.numpy as jnp
from jax import lax
from jax.experimental import pallas as pl
from jax.experimental.pallas import tpu as pltpu
from jax.sharding import PartitionSpec as P

H = 64
KVH = 8
HD = 128
PLEN = 8192
SPAN = 256
SUF = 256
NZ = 8
NX = 4
TASKS = NZ * NX
SHARD = 768
OWN = 32
CHUNK = 160
ROWS = CHUNK * 24
SLOTS = 16
GROUPS = SHARD // 128
LOWEST = -1.0e30
MESH_ID = pl.DeviceIdType.MESH
F32 = jnp.float32
BF16 = jnp.bfloat16
LOG2E = math.log2(math.e)
SCALE = 1.0 / math.sqrt(HD)


class Hop:
    def __init__(self, index, axis, way, dz, dx, low, high, deps):
        self.index, self.axis, self.way = index, axis, way
        self.dz, self.dx, self.low, self.high, self.deps = dz, dx, low, high, deps
        self.kids = []


def gather_tree(split):
    hops = []

    def add(axis, way, dz, dx, rows, deps):
        hop = Hop(len(hops), axis, way, dz, dx, rows[0], rows[1], deps)
        hops.append(hop)
        return hop

    def ring(axis, size, rows, base, dz, dx):
        middle = (rows[0] + rows[1]) // 2
        held = {0: base}
        far = size // 2
        for way in (1, -1):
            deps = base
            for step in range(1, far):
                place = (step * way, dx) if axis == "z" else (dz, step * way)
                deps = [add(axis, way, place[0], place[1], rows, deps)]
                held[step * way] = deps
            half = (rows[0], middle) if way == 1 else (middle, rows[1])
            place = (far, dx) if axis == "z" else (dz, far)
            held.setdefault(far, []).append(add(axis, way, place[0], place[1], half, deps))
        return held

    rows_x, rows_z = (0, split), (split, SHARD)
    for dx, base in ring("x", NX, rows_x, [], 0, 0).items():
        ring("z", NZ, rows_x, base, 0, dx)
    for dz, base in ring("z", NZ, rows_z, [], 0, 0).items():
        ring("x", NX, rows_z, base, dz, 0)
    for hop in hops:
        for dep in hop.deps:
            dep.kids.append(hop)
    free, arrival = {}, {}
    pending = [(0.0, hop.index) for hop in hops if not hop.deps]
    while pending:
        pending.sort()
        ready, index = pending.pop(0)
        hop = hops[index]
        link = (hop.axis, hop.way)
        start = max(ready, free.get(link, 0.0))
        free[link] = start + (hop.high - hop.low) * 256 * 2 / 90e3
        arrival[index] = free[link] + 1.0
        for kid in hop.kids:
            if all(dep.index in arrival for dep in kid.deps):
                pending.append((max(arrival[dep.index] for dep in kid.deps), kid.index))
    return sorted(hops, key=lambda hop: arrival[hop.index])


TREE = gather_tree(320)
BACK = gather_tree(256)


def place():
    task = lax.axis_index("task")
    return task // NX, lax.rem(task, NX)


def task_at(z, x):
    return lax.rem(z + 2 * NZ, NZ) * NX + lax.rem(x + 2 * NX, NX)


def greet(devices):
    barrier = pltpu.get_barrier_semaphore()
    for device in devices:
        pl.semaphore_signal(barrier, inc=1, device_id=device, device_id_type=MESH_ID)
    pl.semaphore_wait(barrier, len(devices))


def plane_neighbours(z, x):
    return [{"task": task_at(z + dz, x + dx)} for dz, dx in ((1, 0), (-1, 0), (0, 1), (0, -1))]


def suffix_pair(pair, q_ref, sk_ref, sv_ref, nk_ref, nv_ref, lens_ref, o_ref, lam_ref):
    q = q_ref[pl.ds(48 * pair, 48), :]
    row = lax.broadcasted_iota(jnp.int32, (48, SUF), 0)
    col = lax.broadcasted_iota(jnp.int32, (48, SUF), 1)
    first = row < 24
    nt = (((1,), (1,)), ((), ()))
    k0 = sk_ref[pl.ds(512 * pair, SUF), :]
    k1 = sk_ref[pl.ds(512 * pair + SUF, SUF), :]
    s0 = lax.dot_general(q, k0, nt, preferred_element_type=F32)
    s1 = lax.dot_general(q, k1, nt, preferred_element_type=F32)
    length = jnp.where(first, lens_ref[2 * pair], lens_ref[2 * pair + 1])
    s = jnp.where(col < length, jnp.where(first, s0, s1) * SCALE, LOWEST)
    f = lax.dot_general(q, nk_ref[...], nt, preferred_element_type=F32) * SCALE
    frow = lax.broadcasted_iota(jnp.int32, (48, 96), 0)
    fcol = lax.broadcasted_iota(jnp.int32, (48, 96), 1)
    later = jnp.where(frow < 24, 0, 1)
    position = (frow - 24 * later) >> 3
    ahead = fcol - 3 * (2 * pair + later)
    f = jnp.where((ahead >= 0) & (ahead <= position), f, LOWEST)
    top = jnp.maximum(jnp.max(s, axis=-1, keepdims=True), jnp.max(f, axis=-1, keepdims=True))
    ws = jnp.exp(s - top)
    wf = jnp.exp(f - top).astype(BF16)
    w0 = jnp.where(first, ws, 0.0).astype(BF16)
    w1 = jnp.where(first, 0.0, ws).astype(BF16)
    total = jnp.sum(w0.astype(F32) + w1.astype(F32), axis=-1, keepdims=True) + jnp.sum(
        wf.astype(F32), axis=-1, keepdims=True
    )
    out = jnp.dot(w0, sv_ref[pl.ds(512 * pair, SUF), :], preferred_element_type=F32)
    out = out + jnp.dot(w1, sv_ref[pl.ds(512 * pair + SUF, SUF), :], preferred_element_type=F32)
    out = out + jnp.dot(wf, nv_ref[...], preferred_element_type=F32)
    o_ref[pl.ds(48 * pair, 48), :] = out / total
    lam_ref[pl.ds(48 * pair, 48), :] = jnp.broadcast_to(top + jnp.log(total), (48, 128))


def gather_kernel(
    q_ref, sk_ref, sv_ref, nk_ref, nv_ref, lens_ref, all_ref, o_ref, lam_ref,
    wide_ref, skv_ref, own_sem, send_sems, recv_sems,
):
    z, x = place()
    loads = []
    for quarter in range(4):
        rows = pl.ds(quarter * 2048, 2048)
        for i, ref in enumerate((sk_ref, sv_ref)):
            load = pltpu.make_async_copy(
                ref.at[rows], skv_ref.at[i, rows], own_sem.at[2 * quarter + i]
            )
            load.start()
            loads.append(load)
    greet(plane_neighbours(z, x))
    own = pltpu.make_async_copy(q_ref, all_ref.at[task_at(z, x)], own_sem.at[8])
    own.start()

    def copy(hop):
        sz, sx = (hop.way, 0) if hop.axis == "z" else (0, hop.way)
        origin = task_at(z - hop.dz + sz, x - hop.dx + sx)
        rows = pl.ds(hop.low, hop.high - hop.low)
        target = all_ref.at[origin, rows]
        return pltpu.make_async_remote_copy(
            src_ref=q_ref.at[rows] if not hop.deps else target,
            dst_ref=target,
            send_sem=send_sems.at[hop.index],
            recv_sem=recv_sems.at[hop.index],
            device_id={"task": task_at(z + sz, x + sx)},
            device_id_type=MESH_ID,
        )

    for hop in TREE:
        if not hop.deps:
            copy(hop).start()
    done = set()
    pair = 0
    for count, hop in enumerate(TREE):
        if count % 4 == 0 and pair < OWN // 2:
            if pair % 4 == 0:
                loads[pair // 2].wait()
                loads[pair // 2 + 1].wait()
            suffix_pair(pair, q_ref, skv_ref.at[0], skv_ref.at[1], nk_ref, nv_ref, lens_ref, o_ref, wide_ref)
            pair += 1
        copy(hop).wait_recv()
        done.add(hop.index)
        for kid in hop.kids:
            if all(dep.index in done for dep in kid.deps):
                copy(kid).start()
    for g in range(GROUPS):
        lam_ref[g] = jnp.transpose(wide_ref[pl.ds(128 * g, 128), :])[0:1, :]
    own.wait()
    for hop in TREE:
        copy(hop).wait_send()


VMEM_SPEC = pl.BlockSpec(memory_space=pltpu.VMEM)
SMEM_SPEC = pl.BlockSpec(memory_space=pltpu.SMEM)
ANY_SPEC = pl.BlockSpec(memory_space=pl.ANY)
HBM_SPEC = pl.BlockSpec(memory_space=pltpu.HBM)


def gather_queries(q, suffix_keys, suffix_values, new_keys, new_values, lens):
    hops = len(TREE)
    return pl.pallas_call(
        gather_kernel,
        out_shape=(
            jax.ShapeDtypeStruct((TASKS, SHARD, HD), BF16),
            jax.ShapeDtypeStruct((SHARD, HD), F32),
            jax.ShapeDtypeStruct((GROUPS, 1, 128), F32),
        ),
        in_specs=[VMEM_SPEC, HBM_SPEC, HBM_SPEC, VMEM_SPEC, VMEM_SPEC, SMEM_SPEC],
        out_specs=(ANY_SPEC, VMEM_SPEC, VMEM_SPEC),
        scratch_shapes=[
            pltpu.VMEM((SHARD, 128), F32),
            pltpu.VMEM((2, OWN * SUF, HD), BF16),
            pltpu.SemaphoreType.DMA((9,)),
            pltpu.SemaphoreType.DMA((hops,)),
            pltpu.SemaphoreType.DMA((hops,)),
        ],
        compiler_params=pltpu.CompilerParams(
            collective_id=0, has_side_effects=True, vmem_limit_bytes=62 * 2**20
        ),
        name="gather_queries",
    )(q, suffix_keys, suffix_values, new_keys, new_values, lens)


def prompt_kernel(
    order_ref, counts_ref, span_ref, q_ref, k_ref, v_ref, out_ref, lam_ref,
    o_ref, wide_ref, qs_ref, acc_ref, top_ref, stage_ref, blocks_ref, have_ref, out_sems,
):
    for p in range(16):
        have_ref[p] = 0
    for slot in range(SLOTS):
        p = span_ref[slot] >> 5
        blocks_ref[p * SLOTS + have_ref[p]] = slot
        have_ref[p] = have_ref[p] + 1

    ones = jnp.ones((SPAN, 128), BF16)
    nt = (((1,), (1,)), ((), ()))

    def fill(first, count):
        def one(i, carry):
            at = pl.multiple_of(order_ref[first + i] * 24, 8)
            o_ref[pl.ds(at, 24), :] = jnp.zeros((24, 128), F32)
            wide_ref[pl.ds(at, 24), :] = jnp.full((24, 128), LOWEST, F32)
            return carry

        lax.fori_loop(0, count, one, 0)

    def chunk(p, base, end, size):
        have = have_ref[p]
        rows = pl.ds(0, 24 * size)
        samples = [order_ref[jnp.minimum(base + i, end - 1)] for i in range(size)]
        for i, s in enumerate(samples):
            at = pl.multiple_of((s >> 1) * 48, 16)
            both = q_ref[pl.ds(at, 48), :].astype(F32)
            qs_ref[pl.ds(24 * i, 24), :] = jnp.where((s & 1) == 1, both[24:48], both[0:24])

        def scores(b):
            at = pl.multiple_of(blocks_ref[p * SLOTS + b] * SPAN, SPAN)
            keys = k_ref[pl.ds(at, SPAN), :]
            values = jnp.concatenate([v_ref[pl.ds(at, SPAN), :], ones], axis=1)
            q = qs_ref[rows, :].astype(BF16)
            return values, lax.dot_general(q, keys, nt, preferred_element_type=F32)

        def weigh(s, top):
            return jnp.exp2((s - top) * (SCALE * LOG2E)).astype(BF16)

        values, s = scores(0)
        top = jnp.max(s, axis=-1, keepdims=True)
        acc_ref[rows, :] = jnp.dot(weigh(s, top), values, preferred_element_type=F32)
        top_ref[rows, :] = jnp.broadcast_to(top, (24 * size, 128))

        def block(b, inner):
            values, s = scores(b)
            old = top_ref[rows, :]
            top = jnp.maximum(old, jnp.max(s, axis=-1, keepdims=True))
            w = weigh(s, jnp.concatenate([top, top], axis=1))
            decay = jnp.exp2((old - top) * (SCALE * LOG2E))
            acc_ref[rows, :] = acc_ref[rows, :] * jnp.concatenate(
                [decay, decay], axis=1
            ) + jnp.dot(w, values, preferred_element_type=F32)
            top_ref[rows, :] = top
            return inner

        lax.fori_loop(1, have, block, 0)
        for i, s in enumerate(samples):
            here = pl.ds(24 * i, 24)
            total = acc_ref[here, pl.ds(128, 128)]
            at = pl.multiple_of(s * 24, 8)
            o_ref[pl.ds(at, 24), :] = acc_ref[here, pl.ds(0, 128)] / total
            wide_ref[pl.ds(at, 24), :] = top_ref[here, :] * SCALE + jnp.log(total)

    def attend(p, first, count):
        full = count // CHUNK

        def whole(c, carry):
            chunk(p, first + c * CHUNK, first + count, CHUNK)
            return carry

        lax.fori_loop(0, full, whole, 0)
        rest = count - full * CHUNK

        @pl.when((rest > 128) & (rest <= 160))
        def _():
            chunk(p, first + full * CHUNK, first + count, 160)

        @pl.when((rest > 96) & (rest <= 128))
        def _():
            chunk(p, first + full * CHUNK, first + count, 128)

        @pl.when((rest > 64) & (rest <= 96))
        def _():
            chunk(p, first + full * CHUNK, first + count, 96)

        @pl.when((rest > 48) & (rest <= 64))
        def _():
            chunk(p, first + full * CHUNK, first + count, 64)

        @pl.when((rest > 32) & (rest <= 48))
        def _():
            chunk(p, first + full * CHUNK, first + count, 48)

        @pl.when((rest > 16) & (rest <= 32))
        def _():
            chunk(p, first + full * CHUNK, first + count, 32)

        @pl.when((rest > 0) & (rest <= 16))
        def _():
            chunk(p, first + full * CHUNK, first + count, 16)

    def prompt(p, first):
        count = counts_ref[p]

        @pl.when(have_ref[p] == 0)
        def _():
            fill(first, count)

        @pl.when(have_ref[p] > 0)
        def _():
            attend(p, first, count)

        return first + count

    lax.fori_loop(0, 16, prompt, 0)

    lane = lax.broadcasted_iota(jnp.int32, (8, 128), 1)
    corner = (lane & 7) == lax.broadcasted_iota(jnp.int32, (8, 128), 0)

    def put(plane):
        tasks = pl.ds(plane * NX, NX)
        return pltpu.make_async_copy(stage_ref.at[tasks], out_ref.at[tasks], out_sems.at[plane])

    def finish(t, carry):
        at = pl.multiple_of(t * SHARD, SHARD)
        stage_ref[t] = o_ref[pl.ds(at, SHARD), :].astype(BF16)

        @pl.when((t & 3) == 3)
        def _():
            put(t >> 2).start()

        for g in range(GROUPS):
            tile = wide_ref[pl.ds(pl.multiple_of(at + 128 * g, 128), 128), :]
            row = tile[0:8]
            for v in range(1, 16):
                row = jnp.where((lane >> 3) == v, tile[8 * v : 8 * v + 8], row)
            lam_ref[t * GROUPS + g] = jnp.sum(jnp.where(corner, row, 0.0), axis=0, keepdims=True)
        return carry

    lax.fori_loop(0, TASKS, finish, 0)
    for plane in range(NZ):
        put(plane).wait()


def attend_prompts(order, counts, spans, q_all, keys, values):
    rows = TASKS * SHARD
    return pl.pallas_call(
        prompt_kernel,
        out_shape=(
            jax.ShapeDtypeStruct((TASKS, SHARD, HD), BF16),
            jax.ShapeDtypeStruct((TASKS * GROUPS, 1, 128), F32),
        ),
        in_specs=[SMEM_SPEC] * 3 + [VMEM_SPEC] * 3,
        out_specs=(HBM_SPEC, VMEM_SPEC),
        scratch_shapes=[
            pltpu.VMEM((rows, 128), F32),
            pltpu.VMEM((rows, 128), F32),
            pltpu.VMEM((ROWS, 128), F32),
            pltpu.VMEM((ROWS, 256), F32),
            pltpu.VMEM((ROWS, 128), F32),
            pltpu.VMEM((TASKS, SHARD, HD), BF16),
            pltpu.SMEM((16 * SLOTS,), jnp.int32),
            pltpu.SMEM((16,), jnp.int32),
            pltpu.SemaphoreType.DMA((NZ,)),
        ],
        compiler_params=pltpu.CompilerParams(vmem_limit_bytes=62 * 2**20),
        cost_estimate=pl.CostEstimate(
            flops=2 * 10**10, bytes_accessed=2 * 10**7, transcendentals=10**7
        ),
        name="attend_prompts",
    )(order, counts, spans, q_all.reshape(rows, HD), keys, values)


def merge_kernel(
    part_in, lam_in, own_ref, own_lam_ref, w0_ref, w1_ref, w2_ref, w3_ref, out_ref,
    part_ref, lam_ref, land_ref, lland_ref, mix_ref, a_ref, p_ref, c_ref, y_ref, yland_ref, mine_ref, r_ref,
    in_sem, send_sems, recv_sems, lsend_sems, lrecv_sems,
    a_sems, c_sems, y_sems, x_sems,
):
    z, x = place()
    tp = lax.axis_index("tp")
    y, core = tp // 2, lax.rem(tp, 2)
    partner = {"tp": 2 * y + 1 - core}
    loads = {}
    for dz in (4, 3, -3, 2, -2, 1, -1, 0):
        plane = pl.ds(task_at(z - dz, 0), NX)
        loads[dz] = pltpu.make_async_copy(
            part_in.at[plane], part_ref.at[plane], in_sem.at[dz + 3]
        )
        loads[dz].start()
    lload = pltpu.make_async_copy(lam_in, lam_ref, in_sem.at[8])
    lload.start()
    greet(plane_neighbours(z, x) + [{"task": task_at(z, x + 2)}, partner]
          + [{"tp": 2 * lax.rem(y + d, 4) + core} for d in (1, 2, 3)])
    lload.wait()
    offsets, at = {}, 0
    for hop in BACK:
        offsets[hop.index] = at
        at += hop.high - hop.low

    def copies(hop):
        origin = task_at(z - hop.dz, x - hop.dx)
        sz, sx = (hop.way, 0) if hop.axis == "z" else (0, hop.way)
        target = {"task": task_at(z - sz, x - sx)}
        size = hop.high - hop.low
        wide = pltpu.make_async_remote_copy(
            src_ref=part_ref.at[origin, pl.ds(hop.low, size)],
            dst_ref=land_ref.at[pl.ds(offsets[hop.index], size)],
            send_sem=send_sems.at[hop.index],
            recv_sem=recv_sems.at[hop.index],
            device_id=target,
            device_id_type=MESH_ID,
        )
        thin = pltpu.make_async_remote_copy(
            src_ref=lam_ref.at[pl.ds(origin * GROUPS + hop.low // 128, size // 128)],
            dst_ref=lland_ref.at[pl.ds(offsets[hop.index] // 128, size // 128)],
            send_sem=lsend_sems.at[hop.index],
            recv_sem=lrecv_sems.at[hop.index],
            device_id=target,
            device_id_type=MESH_ID,
        )
        return thin, wide

    waited = set()

    def merge(origin, low, high, kids, last):
        for hop in kids:
            if hop.index not in waited:
                waited.add(hop.index)
                for copy in copies(hop):
                    copy.wait_recv()
        for g in range(low // 128, high // 128):
            here = [hop for hop in kids if hop.low <= 128 * g < hop.high]
            if not here and not last:
                continue
            lams = [lam_ref[origin * GROUPS + g]]
            parts = [part_ref[origin, pl.ds(128 * g, 128), :].astype(F32)]
            for hop in here:
                start = offsets[hop.index] + 128 * g - hop.low
                lams.append(lland_ref[start // 128])
                parts.append(land_ref[pl.ds(start, 128), :].astype(F32))
            if last:
                lams.append(own_lam_ref[g])
                parts.append(own_ref[pl.ds(128 * g, 128), :])
            top = functools.reduce(jnp.maximum, lams)
            shares = [jnp.exp(lam - top) for lam in lams]
            total = functools.reduce(jnp.add, shares)
            mixed = parts[0]
            for share, part in zip(shares[1:], parts[1:]):
                weight = jnp.transpose(jnp.broadcast_to(share / total, (128, 128)))
                mixed = mixed + weight * (part - parts[0])
            if last:
                mix_ref[pl.ds(128 * g, 128), :] = mixed
            else:
                lam_ref[origin * GROUPS + g] = top + jnp.log(total)
                part_ref[origin, pl.ds(128 * g, 128), :] = mixed.astype(BF16)

    for hop in reversed(BACK):
        if hop.dz in loads:
            loads.pop(hop.dz).wait()
        if hop.kids:
            merge(task_at(z - hop.dz, x - hop.dx), hop.low, hop.high, hop.kids, False)
        for copy in copies(hop):
            copy.start()
    for load in loads.values():
        load.wait()
    merge(task_at(z, x), 0, SHARD, [hop for hop in BACK if not hop.deps], True)
    for hop in BACK:
        for copy in copies(hop):
            copy.wait_send()

    def remote(src, dst, sems, index, device):
        return pltpu.make_async_remote_copy(
            src_ref=src, dst_ref=dst, send_sem=sems.at[0, index], recv_sem=sems.at[1, index],
            device_id=device, device_id_type=MESH_ID,
        )

    for g in range(8):
        a_ref[pl.ds(0, 96), pl.ds(128 * g, 128)] = mix_ref[
            pl.ds(g, 96, stride=8), :
        ].astype(BF16)
    slot_of = {0: 0, 1: 1, -1: 2, 2: 3, -2: 4, 3: 5, -3: 6, 4: 7, -4: 7}

    def row_copy(way, step, half):
        src = pl.ds(96 * slot_of[way * (step - 1)] + 48 * half, 48)
        dst = pl.ds(96 * slot_of[way * step] + 48 * half, 48)
        index = (step - 1) * 4 + (0 if way == 1 else 2) + half
        return remote(
            a_ref.at[src], a_ref.at[dst], a_sems, index, {"task": task_at(z + way, x)}
        )

    hops = [
        (way, step, half)
        for step in range(1, 5)
        for half in (0, 1)
        for way in (1, -1)
        if step < 4 or half == (0 if way == 1 else 1)
    ]

    def block_of(offset):
        return lax.rem(z - offset + NZ, NZ)

    def hand_over(offset):
        block = block_of(offset)
        return lax.rem(block, 2) != core, remote(
            p_ref.at[block], c_ref.at[slot_of[offset]], c_sems, slot_of[offset], partner
        )

    def project(offsets):
        first = slot_of[offsets[0]]
        rows = a_ref[pl.ds(96 * first, 96 * len(offsets)), :]
        for q, w_ref in enumerate((w0_ref, w1_ref, w2_ref, w3_ref)):
            product = jnp.dot(rows, w_ref[...], preferred_element_type=F32)
            for i, offset in enumerate(offsets):
                p_ref[block_of(offset), :, pl.ds(256 * q, 256)] = product[96 * i : 96 * i + 96]
        for offset in offsets:
            away, copy = hand_over(offset)

            @pl.when(away)
            def _():
                copy.start()

    def hand_on(offset):
        block = block_of(offset)
        way = lax.rem(block // 2 - y + 4, 4)
        index = jnp.maximum(way - 1, 0)
        return way > 0, remote(
            y_ref.at[slot_of[offset]], yland_ref.at[index], y_sems, index, {"tp": block}
        )

    def take_over(offsets):
        for offset in offsets:
            away, copy = hand_over(offset)

            @pl.when(jnp.logical_not(away))
            def _():
                copy.wait_recv()
                slot = slot_of[offset]
                total = p_ref[block_of(offset)] + c_ref[slot]
                onward, share = hand_on(offset)

                @pl.when(onward)
                def _():
                    y_ref[slot] = total.astype(BF16)
                    share.start()

                @pl.when(jnp.logical_not(onward))
                def _():
                    mine_ref[...] = total

    for hop in hops:
        if hop[1] == 1:
            row_copy(*hop).start()
    turns = [[0], [1, -1], [2, -2], [3, -3], [4]]
    for step, offsets in enumerate(turns):
        for hop in hops:
            if hop[1] == step:
                row_copy(*hop).wait_recv()
                onward = (hop[0], step + 1, hop[2])
                if onward in hops:
                    row_copy(*onward).start()
        project(offsets)
        if step:
            take_over(turns[step - 1])
    take_over(turns[-1])

    for way in range(3):
        remote(y_ref.at[0], yland_ref.at[way], y_sems, way, partner).wait_recv()
    mine = mine_ref[...]
    for way in range(3):
        mine = mine + yland_ref[way].astype(F32)
    for q in range(NX):
        r_ref[q] = mine[:, 256 * q : 256 * q + 256].astype(BF16)

    shares = []
    for d in (1, 2, 3):
        peer = lax.rem(x + d, NX)
        share = remote(
            r_ref.at[d], out_ref.at[x], x_sems, d - 1, {"task": task_at(z, peer)}
        )
        share.start()
        shares.append(share)
    out_ref[x] = r_ref[0]
    for share in shares:
        share.wait_recv()
    for share in shares:
        share.wait_send()
    for hop in hops:
        row_copy(*hop).wait_send()
    for offset in slot_of:
        if offset > -4:
            away, copy = hand_over(offset)

            @pl.when(away)
            def _():
                copy.wait_send()

            onward, share = hand_on(offset)

            @pl.when(jnp.logical_not(away) & onward)
            def _():
                share.wait_send()


def merge_parts(parts, lams, own, own_lam, weights):
    hops = len(BACK)
    landed = sum(hop.high - hop.low for hop in BACK)
    return pl.pallas_call(
        merge_kernel,
        out_shape=jax.ShapeDtypeStruct((NX, 96, 256), BF16),
        in_specs=[HBM_SPEC, ANY_SPEC] + [VMEM_SPEC] * 6,
        out_specs=VMEM_SPEC,
        scratch_shapes=[
            pltpu.VMEM((TASKS, SHARD, HD), BF16),
            pltpu.VMEM((TASKS * GROUPS, 1, 128), F32),
            pltpu.VMEM((landed, HD), BF16),
            pltpu.VMEM((landed // 128, 1, 128), F32),
            pltpu.VMEM((SHARD, HD), F32),
            pltpu.VMEM((8 * 96, 1024), BF16),
            pltpu.VMEM((8, 96, 1024), F32),
            pltpu.VMEM((8, 96, 1024), F32),
            pltpu.VMEM((8, 96, 1024), BF16),
            pltpu.VMEM((3, 96, 1024), BF16),
            pltpu.VMEM((96, 1024), F32),
            pltpu.VMEM((NX, 96, 256), BF16),
            pltpu.SemaphoreType.DMA((9,)),
            pltpu.SemaphoreType.DMA((hops,)),
            pltpu.SemaphoreType.DMA((hops,)),
            pltpu.SemaphoreType.DMA((hops,)),
            pltpu.SemaphoreType.DMA((hops,)),
            pltpu.SemaphoreType.DMA((2, 16)),
            pltpu.SemaphoreType.DMA((2, 8)),
            pltpu.SemaphoreType.DMA((2, 3)),
            pltpu.SemaphoreType.DMA((2, 3)),
        ],
        compiler_params=pltpu.CompilerParams(
            collective_id=1, has_side_effects=True, vmem_limit_bytes=62 * 2**20
        ),
        name="merge_parts",
    )(parts, lams, own, own_lam, *weights)


def on_device(
    queries, prompt_keys, prompt_values, suffix_keys, suffix_values, new_keys, new_values,
    out_weight, span_perm, share_counts, sample_perm, decoded_lens,
):
    samples = sample_perm.shape[0]
    ids = jnp.arange(samples, dtype=jnp.int32)
    order = jnp.sum(jnp.where(sample_perm[None, :] == ids[:, None], ids[None, :], 0), axis=1)
    q = queries.reshape(SHARD, HD)
    q_all, own, own_lam = gather_queries(
        q, suffix_keys, suffix_values, new_keys, new_values, decoded_lens
    )
    weight, q_all = lax.optimization_barrier((out_weight, q_all))
    weights = [weight]
    for d in (1, 2, 3):
        pairs = [(NX * z + (x + d) % NX, NX * z + x) for z in range(NZ) for x in range(NX)]
        weights.append(lax.ppermute(weight, "task", pairs))
    parts, lams = attend_prompts(order, share_counts, span_perm, q_all, prompt_keys, prompt_values)
    out = merge_parts(parts, lams, own, own_lam, weights)
    return out.reshape(NX * 96, 256).astype(F32)


def solution(mesh):
    return jax.shard_map(
        on_device,
        mesh=mesh,
        in_specs=(
            P("task", "tp"), P("task", "tp"), P("task", "tp"), P("task", "tp"), P("task", "tp"),
            P("task", "tp"), P("task", "tp"), P("tp", "task"), P("task"), P(), P(), P("task"),
        ),
        out_specs=P("tp", "task"),
        check_vma=False,
    )
```
